128 devices in a mesh: grp: 16 (over z_lo, x, core), dev: 8 (over y, z_hi).
Axes of the slice: x: 4, y: 4, z: 4 (z_hi: 2, z_lo: 2; z = z_hi * 2 + z_lo), core: 2. Of those that a mesh axis runs over, the one named last changes fastest.
Arguments:
- inputs: bfloat16 [73728, 1024], P(('grp', 'dev')), may hold values from -6 to 6
- cotangent: bfloat16 [73728, 1024], P(('grp', 'dev')), may hold values from -0.088378906 to 0.088378906
- pre_gelu: bfloat16 [73728, 4096], P(('grp', 'dev')), may hold values from -6 to 6
- w_down: bfloat16 [4096, 1024], P('dev'), may hold values from -0.09375 to 0.09375
- error_feedback: bfloat16 [524288, 1024], P(('grp', 'dev')), may hold values from -0.29882812 to 0.29882812
- a_inverse: bfloat16 [1024, 1024], replicated, as said below
- g_inverse: bfloat16 [4096, 4096], P('dev'), as said below
Outputs:
- preconditioned: float32 [4096, 1024], P('dev')
The draws below stay inside these ranges and needn't reach their ends.
Inputs may be any that keep to these rules, and one draw needn't show every extreme that they name: `a_inverse`: symmetric. `g_inverse`: symmetric.
All inputs are finite; a program needn't handle non-finite values.
Results may differ from the reference program's by a relative error of at most 0.023.
Values may be sent and summed in bfloat16 or wider, within the bound.
No kernel may reach another device: no remote copies, remote signals or barrier semaphores. Data moves between devices by JAX's collectives and lax.ppermute only.
A program may use at most 128 MiB of HBM per device.

```python
import math
import jax
import jax.numpy as jnp
from jax import lax

D = 1024
FF = 4096
TOK_DEV = 576
TOKENS = 73728
N_GRP = 16
N_DEV = 8
DEVICES = 128


def symmetric_factor(noise, diag_part, order, weight):
    off = (noise + noise.T) * (weight / order ** 0.5)
    eye = jnp.eye(order, dtype=jnp.float32)
    return (off * (1.0 - eye) + eye * diag_part[:, None]).astype(jnp.bfloat16)


def draw_a_inverse(key, part):
    key = jax.random.fold_in(key, 11)
    first, second = jax.random.split(key)
    noise = jax.random.normal(first, (D, D), jnp.float32)
    diag_part = jax.random.uniform(second, (D,), jnp.float32, 0.5, 2.0)
    return symmetric_factor(noise, diag_part, D, 0.35)


def draw_g_inverse(key, part):
    key = jax.random.fold_in(key, 23)
    first, second = jax.random.split(key)
    noise = jax.random.normal(first, (FF, FF), jnp.float32)
    diag_part = jax.random.uniform(second, (FF,), jnp.float32, 0.5, 2.0)
    return symmetric_factor(noise, diag_part, FF, 1.2)


def block_levels(own_key, shape, cuts, smallest, top_value):
    loudness = 1.0
    for dim, shards_of in cuts:
        draws = jax.random.uniform(jax.random.fold_in(jax.random.fold_in(own_key, 6), dim), (shards_of,), jnp.float32, smallest / len(cuts), top_value / len(cuts))
        loudness = loudness * jnp.repeat(jnp.exp(draws), shape[dim] // shards_of).reshape((-1,) + (1,) * (len(shape) - 1 - dim))
    return loudness


def scatter_about(rng, extent, scale, reach, cuts=(), kind=jnp.bfloat16):
    array = jax.random.normal(rng, extent, jnp.float32) * scale
    if len(cuts) > 0:
        array = block_levels(rng, extent, cuts, -0.22, 0.18) * array
    return jnp.clip(array, min=-reach, max=reach).astype(kind)


def setup_inputs(seed: int = 0) -> dict:
    streams_of = jax.random.split(jax.random.key(seed), 8)
    return {
        "inputs": scatter_about(streams_of[0], (TOKENS, D), 1.0, 6.0, ((0, 128),)),
        "cotangent": scatter_about(streams_of[1], (TOKENS, D), (4 * TOKENS ** -0.5), 0.088378906, ((0, 128),)),
        "pre_gelu": scatter_about(streams_of[2], (TOKENS, FF), 1.0, 6.0, ((0, 128),)),
        "w_down": scatter_about(streams_of[3], (FF, D), FF ** -0.5, 0.09375, ((0, 8),)),
        "error_feedback": scatter_about(streams_of[4], (DEVICES * FF, D), 0.05, 0.29882812, ((0, 128),)),
        "a_inverse": draw_a_inverse(jax.random.fold_in(streams_of[7], 71), 0),
        "g_inverse": draw_g_inverse(jax.random.fold_in(streams_of[7], 71), 0),
    }


def gelu_slope(value):
    cdf = 0.5 * (1.0 + lax.erf(value * (1.0 / math.sqrt(2.0))))
    density = jnp.exp(-0.5 * value * value) * (1.0 / math.sqrt(2.0 * math.pi))
    return cdf + value * density

def reference(inputs, cotangent, pre_gelu, w_down, error_feedback, a_inverse, g_inverse):
    count = N_GRP * N_DEV
    hi = lax.Precision.HIGHEST
    down_wide = w_down.astype(jnp.float32)
    rows_all = inputs.reshape(count, TOK_DEV, D)
    cot_all = cotangent.reshape(count, TOK_DEV, D)
    pre_all = pre_gelu.reshape(count, TOK_DEV, FF)
    err_all = error_feedback.reshape(count, FF, D)

    def step(total, item):
        rows, cot, pre, err = item
        grad_pre = jnp.dot(cot.astype(jnp.float32), down_wide.T, precision=hi)
        hidden = (grad_pre * gelu_slope(pre.astype(jnp.float32))).astype(jnp.bfloat16)
        part = jnp.dot(hidden.astype(jnp.float32).T, rows.astype(jnp.float32), precision=hi)
        term = (part + err.astype(jnp.float32)).astype(jnp.bfloat16)
        return (total + term.astype(jnp.float32), None)
    grad, _ = lax.scan(step, jnp.zeros((FF, D), jnp.float32), (rows_all, cot_all, pre_all, err_all))
    grad_rounded = grad.astype(jnp.bfloat16)
    right = jnp.dot(grad_rounded, a_inverse, preferred_element_type=jnp.float32).astype(jnp.bfloat16)
    return jnp.dot(g_inverse, right, preferred_element_type=jnp.float32)
```

```python
import functools
import math

import jax
import jax.numpy as jnp
from jax import lax
from jax.experimental import pallas as pl
from jax.experimental.pallas import tpu as pltpu
from jax.sharding import Mesh, PartitionSpec as P

AXES = ("zl", "x", "c", "y", "zh")
SIZES = (2, 4, 2, 4, 2)
BF = jnp.bfloat16
F32 = jnp.float32


def gelu_slope(value):
    cdf = 0.5 * (1.0 + lax.erf(value * (1.0 / math.sqrt(2.0))))
    density = jnp.exp(-0.5 * value * value) * (1.0 / math.sqrt(2.0 * math.pi))
    return cdf + value * density


def slope_kernel(core, pre, out):
    out[...] = gelu_slope(pre[...].astype(F32)).T.astype(BF)


def slopes(core, pre):
    return pl.pallas_call(
        slope_kernel,
        grid_spec=pltpu.PrefetchScalarGridSpec(
            num_scalar_prefetch=1,
            grid=(8,),
            in_specs=[pl.BlockSpec((576, 256), lambda i, s: (0, 2 * i + s[0]))],
            out_specs=pl.BlockSpec((256, 576), lambda i, s: (i, 0)),
        ),
        out_shape=jax.ShapeDtypeStruct((2048, 576), BF),
        cost_estimate=pl.CostEstimate(
            flops=60 * 576 * 2048, bytes_accessed=5 * 2**20, transcendentals=2 * 576 * 2048
        ),
    )(core, pre)


def term_kernel(n, by_columns, place, *refs):
    cot, cot_o, inp, inp_o, slope, slope_o, ef, ef_o = refs[:8]
    ws, outs = refs[8 : 8 + n], refs[8 + n :]
    step = pl.program_id(0)
    w = ws[0][...]
    for i in range(1, n):
        w = jnp.where(step == i, ws[i][...], w)
    hidden = []
    for cots, slope_of in ((cot, slope), (cot_o, slope_o)):
        grad_pre = lax.dot_general(
            w, cots[...], (((1,), (1,)), ((), ())), preferred_element_type=F32
        )
        hidden.append((grad_pre * slope_of[...].astype(F32)).astype(BF))
    for j in range(4):
        if by_columns:
            cols = pl.ds(pl.multiple_of(lax.rem(place[2 * n + 1] + j, 4) * 256, 256), 256)
        else:
            cols = slice(j * 256, (j + 1) * 256)
        total = ef[:, cols].astype(F32) + ef_o[:, cols].astype(F32)
        for h, rows in zip(hidden, (inp, inp_o)):
            total += jnp.dot(h, rows[:, cols], preferred_element_type=F32)
        total = total.astype(BF)
        for k in range(2):
            piece = total[:, k * 128 : (k + 1) * 128]
            if by_columns:
                outs[j][0, k] = piece
            else:
                for i in range(n):

                    @pl.when(step == i)
                    def _():
                        outs[i][2 * j + k] = piece


def terms(by_columns, place, cot, cot_o, inp, inp_o, slope, slope_o, ef, ef_o, ws):
    n = len(ws)
    whole = pl.BlockSpec(cot.shape, lambda i, s: (0, 0))
    block = pl.BlockSpec((256, 1024), lambda i, s: (0, 0))
    slice_of = pl.BlockSpec((256, 576), lambda i, s: (s[i], 0))
    carried = pl.BlockSpec((256, 1024), lambda i, s: (s[i] * 2 + s[2 * n], 0))
    carried_o = pl.BlockSpec((256, 1024), lambda i, s: (s[i], 0))
    if by_columns:
        out_specs = [pl.BlockSpec((1, 2, 256, 128), lambda i, s: (s[n + i], 0, 0, 0))] * 4
        out_shape = [jax.ShapeDtypeStruct((n, 2, 256, 128), BF)] * 4
    else:
        out_specs = [pl.BlockSpec((8, 256, 128), lambda i, s: (0, 0, 0))] * n
        out_shape = [jax.ShapeDtypeStruct((8, 256, 128), BF)] * n
    return pl.pallas_call(
        functools.partial(term_kernel, n, by_columns),
        grid_spec=pltpu.PrefetchScalarGridSpec(
            num_scalar_prefetch=1,
            grid=(n,),
            in_specs=[whole] * 4 + [slice_of] * 2 + [carried, carried_o] + [block] * n,
            out_specs=out_specs,
        ),
        out_shape=out_shape,
        compiler_params=pltpu.CompilerParams(vmem_limit_bytes=60 * 2**20),
        cost_estimate=pl.CostEstimate(
            flops=16 * 1152 * 1024 * 256 * n, bytes_accessed=3 * n * 2**20, transcendentals=0
        ),
    )(place, cot, cot_o, inp, inp_o, slope, slope_o, ef, ef_o, *ws)


def left_kernel(core, g, grads, mine, other, total):
    c, step = core[0], pl.program_id(0)

    @pl.when(step == 0)
    def _():
        total[...] = jnp.zeros_like(total)

    for k in range(2):
        cols = pl.ds(pl.multiple_of(k * 512 + c * 256, 256), 256)
        rows = (grads[k, 0].astype(F32) + grads[1 - k, 1].astype(F32)).astype(BF)
        total[...] += jnp.dot(g[:, cols], rows, preferred_element_type=F32)

    @pl.when(step == 3)
    def _():
        mine[...] = total[pl.ds(pl.multiple_of(c * 256, 256), 256), :]
        other[...] = total[pl.ds(pl.multiple_of((1 - c) * 256, 256), 256), :]


def left_product(core, g, grads):
    rows = pl.BlockSpec((256, 128), lambda i, s: (0, 0))
    return pl.pallas_call(
        left_kernel,
        grid_spec=pltpu.PrefetchScalarGridSpec(
            num_scalar_prefetch=1,
            grid=(4,),
            in_specs=[
                pl.BlockSpec((512, 1024), lambda i, s: (0, i)),
                pl.BlockSpec((2, 2, 256, 128), lambda i, s: (i, 0, 0, 0)),
            ],
            out_specs=[rows, rows],
            scratch_shapes=[pltpu.VMEM((512, 128), F32)],
        ),
        out_shape=[jax.ShapeDtypeStruct((256, 128), F32)] * 2,
        cost_estimate=pl.CostEstimate(
            flops=2 * 512 * 2048 * 128, bytes_accessed=5 * 2**20, transcendentals=0
        ),
    )(core, g, grads)


def shards(inputs, cotangent, pre_gelu, w_down, error_feedback, a_inverse, g_inverse):
    c, y, zh = (lax.axis_index(a) for a in ("c", "y", "zh"))
    x = lax.axis_index("x")
    core = c.astype(jnp.int32).reshape(1)

    def swap(a):
        return lax.ppermute(a, "c", [(0, 1), (1, 0)])

    def across_z(a):
        return lax.ppermute(a, ("zl", "zh"), [(i, 3 - i) for i in range(4)])

    def ring(a, axis, step):
        return lax.ppermute(a, axis, [(i, (i + step) % 4) for i in range(4)])

    w_own = lax.dynamic_slice(w_down, (c * 256, 0), (256, 1024))
    first = [ring(w_own, "y", -1), ring(w_own, "y", 1), swap(pre_gelu)]
    carried = lax.dynamic_index_in_dim(
        error_feedback.reshape(8, 2, 256, 1024), 1 - c, 1, keepdims=False
    ).reshape(2048, 1024)
    w_up, w_low, pre_o, carried, pre, cot, inp, w_own = lax.optimization_barrier(
        (*first, carried, pre_gelu, cotangent, inputs, w_own)
    )
    second = [ring(w_own, "y", 2), across_z(w_own), swap(carried), swap(cot), swap(inp)]
    slope, slope_o = slopes(core, pre), slopes(core, pre_o)
    w_far, w_z, ef_o, cot_o, inp_o, slope, slope_o, w_up, w_low = lax.optimization_barrier(
        (*second, slope, slope_o, w_up, w_low)
    )
    third = [ring(w_z, "y", -1), ring(w_z, "y", 1), across_z(w_far)]

    def product(by_columns, part, ws):
        at = [(lax.rem(y + dy, 4), zh ^ dz) for dy, dz in part]
        place = [a * 2 + b for a, b in at] + [a for a, _ in at] + [c, x]
        return terms(
            by_columns, jnp.stack(place).astype(jnp.int32), cot, cot_o, inp, inp_o,
            slope, slope_o, error_feedback, ef_o, ws,
        )

    def added(parts):
        return sum(p.astype(F32) for p in parts).astype(BF)

    def scattered(a, axes):
        return added(lax.all_to_all(a.reshape(8, 256, 128), axes, 0, 0, tiled=True))

    near = product(True, ((0, 0), (1, 0), (3, 0), (2, 0)), [w_own, w_up, w_low, w_far])
    near, third = lax.optimization_barrier((near, third))
    near = added([near[0]] + [ring(near[j], "x", j) for j in (1, 2, 3)])
    far, up = product(False, ((2, 1), (1, 1)), [third[2], third[0]])
    low, own = product(False, ((3, 1), (0, 1)), [third[1], w_z])
    others = added([own, ring(up, "y", 1), ring(far, "y", 2), ring(low, "y", -1)])
    grad = jnp.stack([scattered(near, ("y", "zl")), scattered(others, ("x", "zl"))])

    grads = lax.all_to_all(
        jnp.broadcast_to(grad[None], (8, 2, 256, 128)), ("y", "zh"), 0, 0, tiled=True
    )
    mine, other = left_product(core, g_inverse, grads)
    left = (mine + swap(other)).astype(BF)
    mine = lax.all_to_all(
        jnp.broadcast_to(left[None], (8, 256, 128)), ("x", "zl"), 0, 0, tiled=True
    ).transpose(1, 0, 2).reshape(256, 1024)
    other = swap(mine)
    both = jnp.where(c == 0, jnp.concatenate([mine, other]), jnp.concatenate([other, mine]))
    return jnp.dot(both, a_inverse, preferred_element_type=F32)


def solution(mesh):
    wide = Mesh(mesh.devices.reshape(SIZES), AXES)
    rows, dev = P(AXES, None), P(("y", "zh"), None)
    return jax.shard_map(
        shards,
        mesh=wide,
        in_specs=(rows, rows, rows, dev, rows, P(), dev),
        out_specs=dev,
        check_vma=False,
    )
```

```python
import functools
import math

import jax
import jax.numpy as jnp
from jax import lax
from jax.experimental import pallas as pl
from jax.experimental.pallas import tpu as pltpu
from jax.sharding import Mesh, PartitionSpec as P

AXES = ("zl", "x", "c", "y", "zh")
SIZES = (2, 4, 2, 4, 2)
BF = jnp.bfloat16
F32 = jnp.float32


def gelu_slope(value):
    cdf = 0.5 * (1.0 + lax.erf(value * (1.0 / math.sqrt(2.0))))
    density = jnp.exp(-0.5 * value * value) * (1.0 / math.sqrt(2.0 * math.pi))
    return cdf + value * density


def prepare_kernel(here, pre, cot, *refs):
    with_ef = len(refs) == 11
    ef, (slope, cot_t), carried = refs[0], refs[with_ef : with_ef + 2], refs[3]
    pre_v, cot_v, ef_v, slope_v, cot_tv, sem, out_sem = refs[-7:]
    c = here[0]

    def start(source, target, semaphore):
        copy = pltpu.make_async_copy(source, target, semaphore)
        copy.start()
        return copy

    reads = [
        start(
            pre.at[:, pl.ds(pl.multiple_of((2 * i + c) * 256, 256), 256)], pre_v.at[i], sem.at[i]
        )
        for i in range(8)
    ]
    reads.append(start(cot, cot_v, sem.at[8]))
    if with_ef:
        for i in range(8):
            rows = pl.ds(pl.multiple_of((2 * i + 1 - c) * 256, 256), 256)
            reads.append(start(ef.at[rows], ef_v.at[i], sem.at[9 + i]))
    writes = []

    def write(source, target):
        writes.append(start(source, target, out_sem.at[len(writes)]))

    for i in range(8):
        reads[i].wait()
        slope_v[i] = gelu_slope(pre_v[i].astype(F32)).astype(BF).T
        write(slope_v.at[i], slope.at[pl.ds(i * 256, 256)])
        if with_ef:
            reads[9 + i].wait()
            write(ef_v.at[i], carried.at[pl.ds(i * 256, 256)])
    reads[8].wait()
    cot_tv[...] = cot_v[...].T
    write(cot_tv, cot_t)
    for copy in writes:
        copy.wait()


def prepare(here, pre, cot, ef=None):
    out_shape = [
        jax.ShapeDtypeStruct((2048, 576), BF),
        jax.ShapeDtypeStruct((1024, 576), BF),
    ]
    args = [here, pre, cot]
    if ef is not None:
        args.append(ef)
        out_shape.append(jax.ShapeDtypeStruct((2048, 1024), BF))
    return pl.pallas_call(
        prepare_kernel,
        in_specs=[pl.BlockSpec(memory_space=pltpu.SMEM)]
        + [pl.BlockSpec(memory_space=pl.ANY)] * (len(args) - 1),
        out_specs=[pl.BlockSpec(memory_space=pl.ANY)] * len(out_shape),
        out_shape=out_shape,
        scratch_shapes=[
            pltpu.VMEM((8, 576, 256), BF),
            pltpu.VMEM((576, 1024), BF),
            pltpu.VMEM((8, 256, 1024), BF),
            pltpu.VMEM((8, 256, 576), BF),
            pltpu.VMEM((1024, 576), BF),
            pltpu.SemaphoreType.DMA((17,)),
            pltpu.SemaphoreType.DMA((17,)),
        ],
        compiler_params=pltpu.CompilerParams(vmem_limit_bytes=60 * 2**20),
        cost_estimate=pl.CostEstimate(
            flops=60 * 576 * 2048, bytes_accessed=5 * 2**20, transcendentals=2 * 576 * 2048
        ),
    )(*args)


def cut_kernel(upper, lower, upper_out, lower_out):
    upper_out[...] = upper[...]
    lower_out[...] = lower[...]


def cut(a, b):
    half = (128, 1024)
    return pl.pallas_call(
        cut_kernel,
        grid=(1,),
        in_specs=[pl.BlockSpec(half, lambda i: (0, 0)), pl.BlockSpec(half, lambda i: (1, 0))],
        out_specs=[pl.BlockSpec(half, lambda i: (0, 0))] * 2,
        out_shape=[jax.ShapeDtypeStruct(half, BF)] * 2,
    )(a, b)


def term_kernel(by_columns, part, here, *refs):
    n = len(part)
    cot, cot_o, inp, inp_o, slope, slope_o, ef, ef_o = refs[:8]
    n_out = 4 if by_columns else n
    ws, outs = refs[8 : 8 + n], refs[8 + n : 8 + n + n_out]
    w_v, cot_v, inp_v, slope_v, ef_v, out_v, sem, out_sem = refs[8 + n + n_out :]
    core, x, y, zh = (here[k] for k in range(4))
    blocks = [lax.rem(y + dy, 4) * 2 + (1 - zh if dz else zh) for dy, dz in part]

    def rows(ref, block):
        return ref.at[pl.ds(pl.multiple_of(block * 256, 256), 256)]

    reads = {}

    def read(name, source, target):
        reads[name] = pltpu.make_async_copy(source, target, sem.at[len(reads)])
        reads[name].start()

    for i in range(n):
        block = blocks[i]
        read(("w", i), ws[i], w_v.at[i])
        if i == 0:
            read("cot", cot, cot_v.at[0])
            read("cot_o", cot_o, cot_v.at[1])
        read(("slope", i), rows(slope, block), slope_v.at[i, 0])
        read(("slope_o", i), rows(slope_o, block), slope_v.at[i, 1])
        if i == 0:
            read("inp", inp, inp_v.at[0])
            read("inp_o", inp_o, inp_v.at[1])
        read(("ef", i), rows(ef, block * 2 + core), ef_v.at[i, 0])
        read(("ef_o", i), rows(ef_o, block), ef_v.at[i, 1])

    writes = []
    for i in range(n):
        reads["w", i].wait()
        hidden = []
        for k, suffix in enumerate(("", "_o")):
            if i == 0:
                reads["cot" + suffix].wait()
            grad_pre = jnp.dot(w_v[i], cot_v[k], preferred_element_type=F32)
            reads["slope" + suffix, i].wait()
            hidden.append((grad_pre * slope_v[i, k].astype(F32)).astype(BF))
        for k, suffix in enumerate(("", "_o")):
            if i == 0:
                reads["inp" + suffix].wait()
            reads["ef" + suffix, i].wait()
        for j in range(4):
            if by_columns:
                cols = pl.ds(pl.multiple_of(lax.rem(x + j, 4) * 256, 256), 256)
            else:
                cols = slice(j * 256, (j + 1) * 256)
            total = ef_v[i, 0, :, cols].astype(F32) + ef_v[i, 1, :, cols].astype(F32)
            for k in range(2):
                total += jnp.dot(hidden[k], inp_v[k, :, cols], preferred_element_type=F32)
            total = total.astype(BF)
            for k in range(2):
                out_v[i, 2 * j + k] = total[:, k * 128 : (k + 1) * 128]
            if by_columns:
                writes.append(
                    pltpu.make_async_copy(
                        out_v.at[i, pl.ds(2 * j, 2)], outs[j].at[lax.rem(y + part[i][0], 4)], out_sem.at[len(writes)]
                    )
                )
                writes[-1].start()
        if not by_columns:
            writes.append(pltpu.make_async_copy(out_v.at[i], outs[i], out_sem.at[i]))
            writes[-1].start()
    for write in writes:
        write.wait()


def terms(by_columns, part, here, cot, cot_o, inp, inp_o, slope, slope_o, ef, ef_o, ws):
    n = len(ws)
    if by_columns:
        out_shape = [jax.ShapeDtypeStruct((n, 2, 256, 128), BF)] * 4
    else:
        out_shape = [jax.ShapeDtypeStruct((8, 256, 128), BF)] * n
    return pl.pallas_call(
        functools.partial(term_kernel, by_columns, part),
        in_specs=[pl.BlockSpec(memory_space=pltpu.SMEM)]
        + [pl.BlockSpec(memory_space=pl.ANY)] * (8 + n),
        out_specs=[pl.BlockSpec(memory_space=pl.ANY)] * len(out_shape),
        out_shape=out_shape,
        scratch_shapes=[
            pltpu.VMEM((n, 256, 1024), BF),
            pltpu.VMEM((2, 1024, 576), BF),
            pltpu.VMEM((2, 576, 1024), BF),
            pltpu.VMEM((n, 2, 256, 576), BF),
            pltpu.VMEM((n, 2, 256, 1024), BF),
            pltpu.VMEM((n, 8, 256, 128), BF),
            pltpu.SemaphoreType.DMA((4 + 5 * n,)),
            pltpu.SemaphoreType.DMA((4 * n if by_columns else n,)),
        ],
        compiler_params=pltpu.CompilerParams(vmem_limit_bytes=60 * 2**20),
        cost_estimate=pl.CostEstimate(
            flops=16 * 1152 * 1024 * 256 * n, bytes_accessed=3 * n * 2**20, transcendentals=0
        ),
    )(here, cot, cot_o, inp, inp_o, slope, slope_o, ef, ef_o, *ws)


def left_kernel(here, g, *refs):
    grads, (mine, other), (g_v, grad_v, total, sem) = refs[:4], refs[4:6], refs[6:]
    c, _, y, zh = (here[k] for k in range(4))
    reads = []
    for i, dy in enumerate((0, 1, 3, 2)):
        for k in range(2):
            block = lax.rem(y + dy, 4) * 2 + (1 - zh if k else zh)
            cols = pl.ds(pl.multiple_of((2 * block + c) * 256, 256), 256)
            reads.append(pltpu.make_async_copy(g.at[:, cols], g_v.at[2 * i + k], sem.at[2 * i + k]))
            reads[-1].start()
    for i in range(4):
        reads.append(pltpu.make_async_copy(grads[i], grad_v.at[i], sem.at[8 + i]))
        reads[-1].start()
    product = 0.0
    for i in range(4):
        reads[8 + i].wait()
        for k in range(2):
            reads[2 * i + k].wait()
            product += jnp.dot(g_v[2 * i + k], grad_v[i, k], preferred_element_type=F32)
    total[...] = product
    mine[...] = total[pl.ds(pl.multiple_of(c * 256, 256), 256), :]
    other[...] = total[pl.ds(pl.multiple_of((1 - c) * 256, 256), 256), :]


def left_product(here, g, grads):
    whole = pl.BlockSpec(memory_space=pltpu.VMEM)
    return pl.pallas_call(
        left_kernel,
        in_specs=[pl.BlockSpec(memory_space=pltpu.SMEM)] + [pl.BlockSpec(memory_space=pl.ANY)] * 5,
        out_specs=[whole, whole],
        out_shape=[jax.ShapeDtypeStruct((256, 128), F32)] * 2,
        scratch_shapes=[
            pltpu.VMEM((8, 512, 256), BF),
            pltpu.VMEM((4, 2, 256, 128), BF),
            pltpu.VMEM((512, 128), F32),
            pltpu.SemaphoreType.DMA((12,)),
        ],
        cost_estimate=pl.CostEstimate(
            flops=2 * 512 * 2048 * 128, bytes_accessed=3 * 2**20, transcendentals=0
        ),
    )(here, g, *grads)


def shards(inputs, cotangent, pre_gelu, w_down, error_feedback, a_inverse, g_inverse):
    c, x, y, zh = (lax.axis_index(a) for a in ("c", "x", "y", "zh"))
    here = jnp.stack([c, x, y, zh]).astype(jnp.int32)

    def swap(a):
        return lax.ppermute(a, "c", [(0, 1), (1, 0)])

    def across_z(a):
        return lax.ppermute(a, ("zl", "zh"), [(i, 3 - i) for i in range(4)])

    def ring(a, axis, step):
        return lax.ppermute(a, axis, [(i, (i + step) % 4) for i in range(4)])

    w_own = lax.dynamic_slice(w_down, (c * 256, 0), (256, 1024))
    first = [ring(w_own, "y", -1), ring(w_own, "y", 1), across_z(w_own)]
    first += [swap(a) for a in (pre_gelu, cotangent)]
    slope, cot, carried = prepare(here, pre_gelu, cotangent, error_feedback)
    w_up, w_low, w_z, pre_o, cot_o, slope, cot, carried, inp = lax.optimization_barrier(
        (*first, slope, cot, carried, inputs)
    )
    upper, lower = cut(w_up, w_low)
    second = [ring(upper, "y", -1), ring(lower, "y", 1), swap(carried), swap(inp)]
    slope_o, cot_o = prepare(here, pre_o, cot_o)
    upper, lower, ef_o, inp_o, slope_o, cot_o, w_up, w_low, w_z = lax.optimization_barrier(
        (*second, slope_o, cot_o, w_up, w_low, w_z)
    )
    w_far = jnp.concatenate([upper, lower])
    third = [ring(w_z, "y", -1), ring(w_z, "y", 1), across_z(w_far)]

    def product(by_columns, part, ws):
        return terms(
            by_columns, part, here, cot, cot_o, inputs, inp_o,
            slope, slope_o, error_feedback, ef_o, ws,
        )

    def added(parts):
        return sum(p.astype(F32) for p in parts).astype(BF)

    def scattered(a, axes):
        return added(lax.all_to_all(a.reshape(8, 256, 128), axes, 0, 0, tiled=True))

    near = product(True, ((0, 0), (1, 0), (3, 0), (2, 0)), [w_own, w_up, w_low, w_far])
    near, third = lax.optimization_barrier((near, third))
    near = added([near[0]] + [ring(near[j], "x", j) for j in (1, 2, 3)])
    far, up, low = product(False, ((2, 1), (1, 1), (3, 1)), [third[2], third[0], third[1]])
    (own,) = product(False, ((0, 1),), [w_z])
    others = added([own, ring(up, "y", 1), ring(far, "y", 2), ring(low, "y", -1)])
    near, others = lax.optimization_barrier((scattered(near, ("y", "zl")), others))
    others = scattered(others, ("x", "zl"))
    theirs = lax.ppermute(jnp.stack([others, near]), "zh", [(0, 1), (1, 0)])
    grad = added([jnp.stack([near, others]), theirs])
    grads = [grad, ring(grad, "y", -1), ring(grad, "y", 1), ring(grad, "y", 2)]
    mine, other = left_product(here, g_inverse, grads)
    left = (mine + swap(other)).astype(BF)
    mine = lax.all_to_all(
        jnp.broadcast_to(left[None], (8, 256, 128)), ("x", "zl"), 0, 0, tiled=True
    ).transpose(1, 0, 2).reshape(256, 1024)
    other = swap(mine)
    both = jnp.where(c == 0, jnp.concatenate([mine, other]), jnp.concatenate([other, mine]))
    return jnp.dot(both, a_inverse, preferred_element_type=F32)


def solution(mesh):
    wide = Mesh(mesh.devices.reshape(SIZES), AXES)
    rows, dev = P(AXES, None), P(("y", "zh"), None)
    return jax.shard_map(
        shards,
        mesh=wide,
        in_specs=(rows, rows, rows, dev, rows, P(), dev),
        out_specs=dev,
        check_vma=False,
    )
```

```python
import functools
import math

import jax
import jax.numpy as jnp
from jax import lax
from jax.experimental import pallas as pl
from jax.experimental.pallas import tpu as pltpu
from jax.sharding import Mesh, PartitionSpec as P

AXES = ("zl", "x", "c", "y", "zh")
SIZES = (2, 4, 2, 4, 2)
BF = jnp.bfloat16
F32 = jnp.float32


def gelu_slope(value):
    cdf = 0.5 * (1.0 + lax.erf(value * (1.0 / math.sqrt(2.0))))
    density = jnp.exp(-0.5 * value * value) * (1.0 / math.sqrt(2.0 * math.pi))
    return cdf + value * density


def prepare_kernel(here, pre, cot, *refs):
    with_ef = len(refs) == 11
    ef, (slope, cot_t), carried = refs[0], refs[with_ef : with_ef + 2], refs[3]
    pre_v, cot_v, ef_v, slope_v, cot_tv, sem, out_sem = refs[-7:]
    c = here[0]

    def start(source, target, semaphore):
        copy = pltpu.make_async_copy(source, target, semaphore)
        copy.start()
        return copy

    reads = [
        start(
            pre.at[:, pl.ds(pl.multiple_of((2 * i + c) * 256, 256), 256)], pre_v.at[i], sem.at[i]
        )
        for i in range(8)
    ]
    reads.append(start(cot, cot_v, sem.at[8]))
    if with_ef:
        for i in range(8):
            rows = pl.ds(pl.multiple_of((2 * i + 1 - c) * 256, 256), 256)
            reads.append(start(ef.at[rows], ef_v.at[i], sem.at[9 + i]))
    writes = []

    def write(source, target):
        writes.append(start(source, target, out_sem.at[len(writes)]))

    for i in range(8):
        reads[i].wait()
        slope_v[i] = gelu_slope(pre_v[i].astype(F32)).astype(BF).T
        write(slope_v.at[i], slope.at[pl.ds(i * 256, 256)])
        if with_ef:
            reads[9 + i].wait()
            write(ef_v.at[i], carried.at[pl.ds(i * 256, 256)])
    reads[8].wait()
    cot_tv[...] = cot_v[...].T
    write(cot_tv, cot_t)
    for copy in writes:
        copy.wait()


def prepare(here, pre, cot, ef=None):
    out_shape = [
        jax.ShapeDtypeStruct((2048, 576), BF),
        jax.ShapeDtypeStruct((1024, 576), BF),
    ]
    args = [here, pre, cot]
    if ef is not None:
        args.append(ef)
        out_shape.append(jax.ShapeDtypeStruct((2048, 1024), BF))
    return pl.pallas_call(
        prepare_kernel,
        in_specs=[pl.BlockSpec(memory_space=pltpu.SMEM)]
        + [pl.BlockSpec(memory_space=pl.ANY)] * (len(args) - 1),
        out_specs=[pl.BlockSpec(memory_space=pl.ANY)] * len(out_shape),
        out_shape=out_shape,
        scratch_shapes=[
            pltpu.VMEM((8, 576, 256), BF),
            pltpu.VMEM((576, 1024), BF),
            pltpu.VMEM((8, 256, 1024), BF),
            pltpu.VMEM((8, 256, 576), BF),
            pltpu.VMEM((1024, 576), BF),
            pltpu.SemaphoreType.DMA((17,)),
            pltpu.SemaphoreType.DMA((17,)),
        ],
        compiler_params=pltpu.CompilerParams(vmem_limit_bytes=60 * 2**20),
        cost_estimate=pl.CostEstimate(
            flops=60 * 576 * 2048, bytes_accessed=5 * 2**20, transcendentals=2 * 576 * 2048
        ),
    )(*args)


def cut_kernel(upper, lower, upper_out, lower_out):
    upper_out[...] = upper[...]
    lower_out[...] = lower[...]


def cut(a, b):
    half = (128, 1024)
    return pl.pallas_call(
        cut_kernel,
        grid=(1,),
        in_specs=[pl.BlockSpec(half, lambda i: (0, 0)), pl.BlockSpec(half, lambda i: (1, 0))],
        out_specs=[pl.BlockSpec(half, lambda i: (0, 0))] * 2,
        out_shape=[jax.ShapeDtypeStruct(half, BF)] * 2,
    )(a, b)


def term_kernel(by_columns, part, here, *refs):
    n = len(part)
    cot, cot_o, inp, inp_o, slope, slope_o, ef, ef_o = refs[:8]
    n_out = 4 if by_columns else n
    ws, outs = refs[8 : -8 - n_out], refs[-8 - n_out : -8]
    w_v, cot_v, inp_v, slope_v, ef_v, out_v, sem, out_sem = refs[-8:]
    core, x, y, zh = (here[k] for k in range(4))
    blocks = [lax.rem(y + dy, 4) * 2 + (1 - zh if dz else zh) for dy, dz in part]

    def rows(ref, block):
        return ref.at[pl.ds(pl.multiple_of(block * 256, 256), 256)]

    reads = {}

    def read(name, source, target):
        reads[name] = pltpu.make_async_copy(source, target, sem.at[len(reads)])
        reads[name].start()

    for i in range(n):
        block = blocks[i]
        halves = i == n - 1 and len(ws) > n
        read(("w", i), ws[i], w_v.at[i, pl.ds(0, 128)] if halves else w_v.at[i])
        if halves:
            read("lower", ws[n], w_v.at[i, pl.ds(128, 128)])
        if i == 0:
            read("cot", cot, cot_v.at[0])
            read("cot_o", cot_o, cot_v.at[1])
        read(("slope", i), rows(slope, block), slope_v.at[i, 0])
        read(("slope_o", i), rows(slope_o, block), slope_v.at[i, 1])
        if i == 0:
            read("inp", inp, inp_v.at[0])
            read("inp_o", inp_o, inp_v.at[1])
        read(("ef", i), rows(ef, block * 2 + core), ef_v.at[i, 0])
        read(("ef_o", i), rows(ef_o, block), ef_v.at[i, 1])

    writes = []
    for i in range(n):
        reads["w", i].wait()
        if i == n - 1 and len(ws) > n:
            reads["lower"].wait()
        hidden = []
        for k, suffix in enumerate(("", "_o")):
            if i == 0:
                reads["cot" + suffix].wait()
            grad_pre = jnp.dot(w_v[i], cot_v[k], preferred_element_type=F32)
            reads["slope" + suffix, i].wait()
            hidden.append((grad_pre * slope_v[i, k].astype(F32)).astype(BF))
        for k, suffix in enumerate(("", "_o")):
            if i == 0:
                reads["inp" + suffix].wait()
            reads["ef" + suffix, i].wait()
        for j in range(4):
            if by_columns:
                cols = pl.ds(pl.multiple_of(lax.rem(x + j, 4) * 256, 256), 256)
            else:
                cols = slice(j * 256, (j + 1) * 256)
            total = ef_v[i, 0, :, cols].astype(F32) + ef_v[i, 1, :, cols].astype(F32)
            for k in range(2):
                total += jnp.dot(hidden[k], inp_v[k, :, cols], preferred_element_type=F32)
            total = total.astype(BF)
            for k in range(2):
                out_v[i, 2 * j + k] = total[:, k * 128 : (k + 1) * 128]
            if by_columns:
                writes.append(
                    pltpu.make_async_copy(
                        out_v.at[i, pl.ds(2 * j, 2)], outs[j].at[lax.rem(y + part[i][0], 4)], out_sem.at[len(writes)]
                    )
                )
                writes[-1].start()
        if not by_columns:
            writes.append(pltpu.make_async_copy(out_v.at[i], outs[i], out_sem.at[i]))
            writes[-1].start()
    for write in writes:
        write.wait()


def terms(by_columns, part, here, cot, cot_o, inp, inp_o, slope, slope_o, ef, ef_o, ws):
    n = len(part)
    if by_columns:
        out_shape = [jax.ShapeDtypeStruct((n, 2, 256, 128), BF)] * 4
    else:
        out_shape = [jax.ShapeDtypeStruct((8, 256, 128), BF)] * n
    return pl.pallas_call(
        functools.partial(term_kernel, by_columns, part),
        in_specs=[pl.BlockSpec(memory_space=pltpu.SMEM)]
        + [pl.BlockSpec(memory_space=pl.ANY)] * (8 + len(ws)),
        out_specs=[pl.BlockSpec(memory_space=pl.ANY)] * len(out_shape),
        out_shape=out_shape,
        scratch_shapes=[
            pltpu.VMEM((n, 256, 1024), BF),
            pltpu.VMEM((2, 1024, 576), BF),
            pltpu.VMEM((2, 576, 1024), BF),
            pltpu.VMEM((n, 2, 256, 576), BF),
            pltpu.VMEM((n, 2, 256, 1024), BF),
            pltpu.VMEM((n, 8, 256, 128), BF),
            pltpu.SemaphoreType.DMA((5 + 5 * n,)),
            pltpu.SemaphoreType.DMA((4 * n if by_columns else n,)),
        ],
        compiler_params=pltpu.CompilerParams(vmem_limit_bytes=60 * 2**20),
        cost_estimate=pl.CostEstimate(
            flops=(16 if n == 4 else 4) * 1152 * 1024 * 256 * n, bytes_accessed=3 * n * 2**20, transcendentals=0
        ),
    )(here, cot, cot_o, inp, inp_o, slope, slope_o, ef, ef_o, *ws)


def columns_kernel(here, g, out, sem):
    c, _, y, zh = (here[k] for k in range(4))
    copies = []
    for i, dy in enumerate((0, 1, 3, 2)):
        for k in range(2):
            block = lax.rem(y + dy, 4) * 2 + (1 - zh if k else zh)
            cols = pl.ds(pl.multiple_of((2 * block + c) * 256, 256), 256)
            n = 2 * i + k
            copies.append(
                pltpu.make_async_copy(
                    g.at[:, cols], out.at[:, n * 256 : (n + 1) * 256], sem.at[n]
                )
            )
            copies[-1].start()
    for copy in copies:
        copy.wait()


def own_columns(here, g):
    return pl.pallas_call(
        columns_kernel,
        in_specs=[pl.BlockSpec(memory_space=pltpu.SMEM), pl.BlockSpec(memory_space=pl.ANY)],
        out_specs=pl.BlockSpec(memory_space=pltpu.VMEM),
        out_shape=jax.ShapeDtypeStruct((512, 2048), BF),
        scratch_shapes=[pltpu.SemaphoreType.DMA((8,))],
        cost_estimate=pl.CostEstimate(flops=0, bytes_accessed=4 * 2**20, transcendentals=0),
    )(here, g)


def shards(inputs, cotangent, pre_gelu, w_down, error_feedback, a_inverse, g_inverse):
    c, x, y, zh = (lax.axis_index(a) for a in ("c", "x", "y", "zh"))
    here = jnp.stack([c, x, y, zh]).astype(jnp.int32)

    def swap(a):
        return lax.ppermute(a, "c", [(0, 1), (1, 0)])

    def across_z(a):
        return lax.ppermute(a, ("zl", "zh"), [(i, 3 - i) for i in range(4)])

    def ring(a, axis, step):
        return lax.ppermute(a, axis, [(i, (i + step) % 4) for i in range(4)])

    w_own = lax.dynamic_slice(w_down, (c * 256, 0), (256, 1024))
    first = [ring(w_own, "y", -1), ring(w_own, "y", 1), across_z(w_own)]
    first += [swap(a) for a in (pre_gelu, cotangent)]
    slope, cot, carried = prepare(here, pre_gelu, cotangent, error_feedback)
    g_half = own_columns(here, g_inverse)
    w_up, w_low, w_z, pre_o, cot_o, slope, cot, carried, inp, g_half = lax.optimization_barrier(
        (*first, slope, cot, carried, inputs, g_half)
    )
    upper, lower = cut(w_up, w_low)
    second = [ring(upper, "y", -1), ring(lower, "y", 1), swap(carried), swap(inp)]
    slope_o, cot_o = prepare(here, pre_o, cot_o)
    upper, lower, ef_o, inp_o, slope_o, cot_o, w_up, w_low, w_z = lax.optimization_barrier(
        (*second, slope_o, cot_o, w_up, w_low, w_z)
    )
    third = [ring(w_z, "y", -1), ring(w_z, "y", 1), across_z(upper), across_z(lower)]

    def product(by_columns, part, ws):
        return terms(
            by_columns, part, here, cot, cot_o, inputs, inp_o,
            slope, slope_o, error_feedback, ef_o, ws,
        )

    def added(parts):
        return sum(p.astype(F32) for p in parts).astype(BF)

    def exchanged(a, axes):
        return lax.all_to_all(a.reshape(8, 256, 128), axes, 0, 0, tiled=True)

    near = product(True, ((0, 0), (1, 0), (3, 0), (2, 0)), [w_own, w_up, w_low, upper, lower])
    near, third = lax.optimization_barrier((near, third))
    near = added([near[0]] + [ring(near[j], "x", j) for j in (1, 2, 3)])
    (far,) = product(False, ((2, 1),), third[2:])
    up, low = product(False, ((1, 1), (3, 1)), [third[0], third[1]])
    (own,) = product(False, ((0, 1),), [w_z])
    others = added([own, ring(up, "y", 1), ring(far, "y", 2), ring(low, "y", -1)])
    near, others = lax.optimization_barrier((exchanged(near, ("y", "zl")), others))
    near, others = added(near), added(exchanged(others, ("x", "zl")))
    theirs = lax.ppermute(jnp.stack([others, near]), "zh", [(0, 1), (1, 0)])
    grad = added([jnp.stack([near, others]), theirs])
    grads = [grad, ring(grad, "y", -1), ring(grad, "y", 1), ring(grad, "y", 2)]
    part = jnp.dot(
        g_half, jnp.concatenate(grads).reshape(2048, 128), preferred_element_type=F32
    ).reshape(2, 256, 128)
    mine, other = (lax.dynamic_index_in_dim(part, k, 0, keepdims=False) for k in (c, 1 - c))
    left = (mine + swap(other)).astype(BF)
    mine = lax.all_to_all(
        jnp.broadcast_to(left[None], (8, 256, 128)), ("x", "zl"), 0, 0, tiled=True
    ).transpose(1, 0, 2).reshape(256, 1024)
    other = swap(mine)
    both = jnp.where(c == 0, jnp.concatenate([mine, other]), jnp.concatenate([other, mine]))
    return jnp.dot(both, a_inverse, preferred_element_type=F32)


def solution(mesh):
    wide = Mesh(mesh.devices.reshape(SIZES), AXES)
    rows, dev = P(AXES, None), P(("y", "zh"), None)
    return jax.shard_map(
        shards,
        mesh=wide,
        in_specs=(rows, rows, rows, dev, rows, P(), dev),
        out_specs=dev,
        check_vma=False,
    )
```

```python
import functools
import math

import jax
import jax.numpy as jnp
from jax import lax
from jax.experimental import pallas as pl
from jax.experimental.pallas import tpu as pltpu
from jax.sharding import Mesh, PartitionSpec as P

AXES = ("zl", "x", "c", "y", "zh")
SIZES = (2, 4, 2, 4, 2)
BF = jnp.bfloat16
F32 = jnp.float32


def gelu_slope(value):
    cdf = 0.5 * (1.0 + lax.erf(value * (1.0 / math.sqrt(2.0))))
    density = jnp.exp(-0.5 * value * value) * (1.0 / math.sqrt(2.0 * math.pi))
    return cdf + value * density


def prepare_kernel(here, pre, cot, *refs):
    with_ef = len(refs) == 11
    ef, (slope, cot_t), carried = refs[0], refs[with_ef : with_ef + 2], refs[3]
    pre_v, cot_v, ef_v, slope_v, cot_tv, sem, out_sem = refs[-7:]
    c = here[0]

    def start(source, target, semaphore):
        copy = pltpu.make_async_copy(source, target, semaphore)
        copy.start()
        return copy

    reads = [
        start(
            pre.at[:, pl.ds(pl.multiple_of((2 * i + c) * 256, 256), 256)], pre_v.at[i], sem.at[i]
        )
        for i in range(8)
    ]
    reads.append(start(cot, cot_v, sem.at[8]))
    if with_ef:
        for i in range(8):
            rows = pl.ds(pl.multiple_of((2 * i + 1 - c) * 256, 256), 256)
            reads.append(start(ef.at[rows], ef_v.at[i], sem.at[9 + i]))
    writes = []

    def write(source, target):
        writes.append(start(source, target, out_sem.at[len(writes)]))

    for i in range(8):
        reads[i].wait()
        slope_v[i] = gelu_slope(pre_v[i].astype(F32)).astype(BF).T
        write(slope_v.at[i], slope.at[pl.ds(i * 256, 256)])
        if with_ef:
            reads[9 + i].wait()
            write(ef_v.at[i], carried.at[pl.ds(i * 256, 256)])
    reads[8].wait()
    cot_tv[...] = cot_v[...].T
    write(cot_tv, cot_t)
    for copy in writes:
        copy.wait()


def prepare(here, pre, cot, ef=None):
    out_shape = [
        jax.ShapeDtypeStruct((2048, 576), BF),
        jax.ShapeDtypeStruct((1024, 576), BF),
    ]
    args = [here, pre, cot]
    if ef is not None:
        args.append(ef)
        out_shape.append(jax.ShapeDtypeStruct((2048, 1024), BF))
    return pl.pallas_call(
        prepare_kernel,
        in_specs=[pl.BlockSpec(memory_space=pltpu.SMEM)]
        + [pl.BlockSpec(memory_space=pl.ANY)] * (len(args) - 1),
        out_specs=[pl.BlockSpec(memory_space=pl.ANY)] * len(out_shape),
        out_shape=out_shape,
        scratch_shapes=[
            pltpu.VMEM((8, 576, 256), BF),
            pltpu.VMEM((576, 1024), BF),
            pltpu.VMEM((8, 256, 1024), BF),
            pltpu.VMEM((8, 256, 576), BF),
            pltpu.VMEM((1024, 576), BF),
            pltpu.SemaphoreType.DMA((17,)),
            pltpu.SemaphoreType.DMA((17,)),
        ],
        compiler_params=pltpu.CompilerParams(vmem_limit_bytes=60 * 2**20),
        cost_estimate=pl.CostEstimate(
            flops=60 * 576 * 2048, bytes_accessed=5 * 2**20, transcendentals=2 * 576 * 2048
        ),
    )(*args)


def cut_kernel(upper, lower, upper_out, lower_out):
    upper_out[...] = upper[...]
    lower_out[...] = lower[...]


def cut(a, b):
    half = (128, 1024)
    return pl.pallas_call(
        cut_kernel,
        grid=(1,),
        in_specs=[pl.BlockSpec(half, lambda i: (0, 0)), pl.BlockSpec(half, lambda i: (1, 0))],
        out_specs=[pl.BlockSpec(half, lambda i: (0, 0))] * 2,
        out_shape=[jax.ShapeDtypeStruct(half, BF)] * 2,
    )(a, b)


def term_kernel(by_columns, part, here, *refs):
    n = len(part)
    cot, cot_o, inp, inp_o, slope, slope_o, ef, ef_o = refs[:8]
    n_out = 1 if by_columns else n
    ws, outs = refs[8 : -8 - n_out], refs[-8 - n_out : -8]
    w_v, cot_v, inp_v, slope_v, ef_v, out_v, sem, out_sem = refs[-8:]
    core, _, y, zh = (here[k] for k in range(4))
    blocks = [lax.rem(y + dy, 4) * 2 + (1 - zh if dz else zh) for dy, dz in part]

    def rows(ref, block):
        return ref.at[pl.ds(pl.multiple_of(block * 256, 256), 256)]

    reads = {}

    def read(name, source, target):
        reads[name] = pltpu.make_async_copy(source, target, sem.at[len(reads)])
        reads[name].start()

    for i in range(n):
        block = blocks[i]
        halves = i == n - 1 and len(ws) > n
        read(("w", i), ws[i], w_v.at[i, pl.ds(0, 128)] if halves else w_v.at[i])
        if halves:
            read("lower", ws[n], w_v.at[i, pl.ds(128, 128)])
        if i == 0:
            read("cot", cot, cot_v.at[0])
            read("cot_o", cot_o, cot_v.at[1])
        read(("slope", i), rows(slope, block), slope_v.at[i, 0])
        read(("slope_o", i), rows(slope_o, block), slope_v.at[i, 1])
        if i == 0:
            read("inp", inp, inp_v.at[0])
            read("inp_o", inp_o, inp_v.at[1])
        read(("ef", i), rows(ef, block * 2 + core), ef_v.at[i, 0])
        read(("ef_o", i), rows(ef_o, block), ef_v.at[i, 1])

    writes = []
    for i in range(n):
        reads["w", i].wait()
        if i == n - 1 and len(ws) > n:
            reads["lower"].wait()
        hidden = []
        for k, suffix in enumerate(("", "_o")):
            if i == 0:
                reads["cot" + suffix].wait()
            grad_pre = jnp.dot(w_v[i], cot_v[k], preferred_element_type=F32)
            reads["slope" + suffix, i].wait()
            hidden.append((grad_pre * slope_v[i, k].astype(F32)).astype(BF))
        for k, suffix in enumerate(("", "_o")):
            if i == 0:
                reads["inp" + suffix].wait()
            reads["ef" + suffix, i].wait()
        for j in range(4):
            cols = slice(j * 256, (j + 1) * 256)
            total = ef_v[i, 0, :, cols].astype(F32) + ef_v[i, 1, :, cols].astype(F32)
            for k in range(2):
                total += jnp.dot(hidden[k], inp_v[k, :, cols], preferred_element_type=F32)
            total = total.astype(BF)
            for k in range(2):
                out_v[i, 2 * j + k] = total[:, k * 128 : (k + 1) * 128]
            if by_columns:
                writes.append(
                    pltpu.make_async_copy(
                        out_v.at[i, pl.ds(2 * j, 2)], outs[0].at[j, pl.ds(0, 2), i], out_sem.at[len(writes)]
                    )
                )
                writes[-1].start()
        if not by_columns:
            writes.append(pltpu.make_async_copy(out_v.at[i], outs[i], out_sem.at[i]))
            writes[-1].start()
    for write in writes:
        write.wait()


def terms(by_columns, part, here, cot, cot_o, inp, inp_o, slope, slope_o, ef, ef_o, ws):
    n = len(part)
    if by_columns:
        out_shape = [jax.ShapeDtypeStruct((4, 2, n, 256, 128), BF)]
    else:
        out_shape = [jax.ShapeDtypeStruct((8, 256, 128), BF)] * n
    return pl.pallas_call(
        functools.partial(term_kernel, by_columns, part),
        in_specs=[pl.BlockSpec(memory_space=pltpu.SMEM)]
        + [pl.BlockSpec(memory_space=pl.ANY)] * (8 + len(ws)),
        out_specs=[pl.BlockSpec(memory_space=pl.ANY)] * len(out_shape),
        out_shape=out_shape,
        scratch_shapes=[
            pltpu.VMEM((n, 256, 1024), BF),
            pltpu.VMEM((2, 1024, 576), BF),
            pltpu.VMEM((2, 576, 1024), BF),
            pltpu.VMEM((n, 2, 256, 576), BF),
            pltpu.VMEM((n, 2, 256, 1024), BF),
            pltpu.VMEM((n, 8, 256, 128), BF),
            pltpu.SemaphoreType.DMA((5 + 5 * n,)),
            pltpu.SemaphoreType.DMA((4 * n if by_columns else n,)),
        ],
        compiler_params=pltpu.CompilerParams(vmem_limit_bytes=60 * 2**20),
        cost_estimate=pl.CostEstimate(
            flops=(16 if n == 4 else 4) * 1152 * 1024 * 256 * n, bytes_accessed=3 * n * 2**20, transcendentals=0
        ),
    )(here, cot, cot_o, inp, inp_o, slope, slope_o, ef, ef_o, *ws)


def columns_kernel(here, g, out, sem):
    c, _, y, zh = (here[k] for k in range(4))
    copies = []
    for i, dy in enumerate((0, 1, 3, 2)):
        for k in range(2):
            block = lax.rem(y + dy, 4) * 2 + (1 - zh if k else zh)
            cols = pl.ds(pl.multiple_of((2 * block + c) * 256, 256), 256)
            n = 2 * i + k
            copies.append(
                pltpu.make_async_copy(
                    g.at[:, cols], out.at[:, n * 256 : (n + 1) * 256], sem.at[n]
                )
            )
            copies[-1].start()
    for copy in copies:
        copy.wait()


def own_columns(here, g):
    return pl.pallas_call(
        columns_kernel,
        in_specs=[pl.BlockSpec(memory_space=pltpu.SMEM), pl.BlockSpec(memory_space=pl.ANY)],
        out_specs=pl.BlockSpec(memory_space=pltpu.VMEM),
        out_shape=jax.ShapeDtypeStruct((512, 2048), BF),
        scratch_shapes=[pltpu.SemaphoreType.DMA((8,))],
        cost_estimate=pl.CostEstimate(flops=0, bytes_accessed=4 * 2**20, transcendentals=0),
    )(here, g)


def shards(inputs, cotangent, pre_gelu, w_down, error_feedback, a_inverse, g_inverse):
    c, x, y, zh, zl = (lax.axis_index(a) for a in ("c", "x", "y", "zh", "zl"))
    here = jnp.stack([c, x, y, zh]).astype(jnp.int32)

    def swap(a):
        return lax.ppermute(a, "c", [(0, 1), (1, 0)])

    def across_z(a):
        return lax.ppermute(a, ("zl", "zh"), [(i, 3 - i) for i in range(4)])

    def ring(a, axis, step):
        return lax.ppermute(a, axis, [(i, (i + step) % 4) for i in range(4)])

    w_own = lax.dynamic_slice(w_down, (c * 256, 0), (256, 1024))
    first = [ring(w_own, "y", -1), ring(w_own, "y", 1), across_z(w_own)]
    first += [swap(a) for a in (pre_gelu, cotangent)]
    slope, cot, carried = prepare(here, pre_gelu, cotangent, error_feedback)
    g_half = own_columns(here, g_inverse)
    w_up, w_low, w_z, pre_o, cot_o, slope, cot, carried, inp, g_half = lax.optimization_barrier(
        (*first, slope, cot, carried, inputs, g_half)
    )
    upper, lower = cut(w_up, w_low)
    second = [ring(upper, "y", -1), ring(lower, "y", 1), swap(carried), swap(inp)]
    slope_o, cot_o = prepare(here, pre_o, cot_o)
    upper, lower, ef_o, inp_o, slope_o, cot_o, w_up, w_low, w_z = lax.optimization_barrier(
        (*second, slope_o, cot_o, w_up, w_low, w_z)
    )
    third = [ring(w_z, "y", -1), ring(w_z, "y", 1), across_z(upper), across_z(lower)]

    def product(by_columns, part, ws):
        return terms(
            by_columns, part, here, cot, cot_o, inputs, inp_o,
            slope, slope_o, error_feedback, ef_o, ws,
        )

    def added(parts):
        return sum(p.astype(F32) for p in parts).astype(BF)

    def half(a, which):
        return lax.dynamic_index_in_dim(a, which, 0, keepdims=False)

    def exchanged(a, axes):
        return lax.all_to_all(a.reshape(8, 256, 128), axes, 0, 0, tiled=True)

    (near,) = product(True, ((0, 0), (1, 0), (3, 0), (2, 0)), [w_own, w_up, w_low, upper, lower])
    near, third = lax.optimization_barrier((near, third))
    near = added(lax.all_to_all(near, "x", 0, 0, tiled=True))
    near = added([half(near, zl), lax.ppermute(half(near, 1 - zl), "zl", [(0, 1), (1, 0)])])
    near = added([near[0], ring(near[1], "y", 1), ring(near[2], "y", -1), ring(near[3], "y", 2)])
    (far,) = product(False, ((2, 1),), third[2:])
    up, low = product(False, ((1, 1), (3, 1)), [third[0], third[1]])
    (own,) = product(False, ((0, 1),), [w_z])
    others = added([own, ring(up, "y", 1), ring(far, "y", 2), ring(low, "y", -1)])
    others = added(exchanged(others, ("x", "zl")))
    theirs = lax.ppermute(jnp.stack([others, near]), "zh", [(0, 1), (1, 0)])
    grad = added([jnp.stack([near, others]), theirs])
    grads = [grad, ring(grad, "y", -1), ring(grad, "y", 1), ring(grad, "y", 2)]
    part = jnp.dot(
        g_half, jnp.concatenate(grads).reshape(2048, 128), preferred_element_type=F32
    ).reshape(2, 256, 128)
    mine, other = (lax.dynamic_index_in_dim(part, k, 0, keepdims=False) for k in (c, 1 - c))
    left = (mine + swap(other)).astype(BF)
    mine = lax.all_to_all(
        jnp.broadcast_to(left[None], (8, 256, 128)), ("x", "zl"), 0, 0, tiled=True
    ).transpose(1, 0, 2).reshape(256, 1024)
    other = swap(mine)
    both = jnp.where(c == 0, jnp.concatenate([mine, other]), jnp.concatenate([other, mine]))
    return jnp.dot(both, a_inverse, preferred_element_type=F32)


def solution(mesh):
    wide = Mesh(mesh.devices.reshape(SIZES), AXES)
    rows, dev = P(AXES, None), P(("y", "zh"), None)
    return jax.shard_map(
        shards,
        mesh=wide,
        in_specs=(rows, rows, rows, dev, rows, P(), dev),
        out_specs=dev,
        check_vma=False,
    )
```

```python
import functools
import math

import jax
import jax.numpy as jnp
from jax import lax
from jax.experimental import pallas as pl
from jax.experimental.pallas import tpu as pltpu
from jax.sharding import Mesh, PartitionSpec as P

AXES = ("zl", "x", "c", "y", "zh")
SIZES = (2, 4, 2, 4, 2)
BF = jnp.bfloat16
F32 = jnp.float32


def gelu_slope(value):
    cdf = 0.5 * (1.0 + lax.erf(value * (1.0 / math.sqrt(2.0))))
    density = jnp.exp(-0.5 * value * value) * (1.0 / math.sqrt(2.0 * math.pi))
    return cdf + value * density


def prepare_kernel(here, pre, cot, *refs):
    with_ef = len(refs) == 11
    ef, (slope, cot_t), carried = refs[0], refs[with_ef : with_ef + 2], refs[3]
    pre_v, cot_v, ef_v, slope_v, cot_tv, sem, out_sem = refs[-7:]
    c = here[0]

    def start(source, target, semaphore):
        copy = pltpu.make_async_copy(source, target, semaphore)
        copy.start()
        return copy

    reads = [
        start(
            pre.at[:, pl.ds(pl.multiple_of((2 * i + c) * 256, 256), 256)], pre_v.at[i], sem.at[i]
        )
        for i in range(8)
    ]
    reads.append(start(cot, cot_v, sem.at[8]))
    if with_ef:
        for i in range(8):
            rows = pl.ds(pl.multiple_of((2 * i + 1 - c) * 256, 256), 256)
            reads.append(start(ef.at[rows], ef_v.at[i], sem.at[9 + i]))
    writes = []

    def write(source, target):
        writes.append(start(source, target, out_sem.at[len(writes)]))

    for i in range(8):
        reads[i].wait()
        slope_v[i] = gelu_slope(pre_v[i].astype(F32)).astype(BF).T
        write(slope_v.at[i], slope.at[pl.ds(i * 256, 256)])
        if with_ef:
            reads[9 + i].wait()
            write(ef_v.at[i], carried.at[pl.ds(i * 256, 256)])
    reads[8].wait()
    cot_tv[...] = cot_v[...].T
    write(cot_tv, cot_t)
    for copy in writes:
        copy.wait()


def prepare(here, pre, cot, ef=None):
    out_shape = [
        jax.ShapeDtypeStruct((2048, 576), BF),
        jax.ShapeDtypeStruct((1024, 576), BF),
    ]
    args = [here, pre, cot]
    if ef is not None:
        args.append(ef)
        out_shape.append(jax.ShapeDtypeStruct((2048, 1024), BF))
    return pl.pallas_call(
        prepare_kernel,
        in_specs=[pl.BlockSpec(memory_space=pltpu.SMEM)]
        + [pl.BlockSpec(memory_space=pl.ANY)] * (len(args) - 1),
        out_specs=[pl.BlockSpec(memory_space=pl.ANY)] * len(out_shape),
        out_shape=out_shape,
        scratch_shapes=[
            pltpu.VMEM((8, 576, 256), BF),
            pltpu.VMEM((576, 1024), BF),
            pltpu.VMEM((8, 256, 1024), BF),
            pltpu.VMEM((8, 256, 576), BF),
            pltpu.VMEM((1024, 576), BF),
            pltpu.SemaphoreType.DMA((17,)),
            pltpu.SemaphoreType.DMA((17,)),
        ],
        compiler_params=pltpu.CompilerParams(vmem_limit_bytes=60 * 2**20),
        cost_estimate=pl.CostEstimate(
            flops=60 * 576 * 2048, bytes_accessed=5 * 2**20, transcendentals=2 * 576 * 2048
        ),
    )(*args)


def cut_kernel(upper, lower, upper_out, lower_out):
    upper_out[...] = upper[...]
    lower_out[...] = lower[...]


def cut(a, b):
    half = (128, 1024)
    return pl.pallas_call(
        cut_kernel,
        grid=(1,),
        in_specs=[pl.BlockSpec(half, lambda i: (0, 0)), pl.BlockSpec(half, lambda i: (1, 0))],
        out_specs=[pl.BlockSpec(half, lambda i: (0, 0))] * 2,
        out_shape=[jax.ShapeDtypeStruct(half, BF)] * 2,
    )(a, b)


def term_kernel(by_columns, part, here, *refs):
    n = len(part)
    cot, cot_o, inp, inp_o, slope, slope_o, ef, ef_o = refs[:8]
    n_out = 1 if by_columns else n
    ws, outs = refs[8 : -8 - n_out], refs[-8 - n_out : -8]
    w_v, cot_v, inp_v, slope_v, ef_v, out_v, sem, out_sem = refs[-8:]
    core, _, y, zh = (here[k] for k in range(4))
    blocks = [lax.rem(y + dy, 4) * 2 + (1 - zh if dz else zh) for dy, dz in part]

    def rows(ref, block):
        return ref.at[pl.ds(pl.multiple_of(block * 256, 256), 256)]

    reads = {}

    def read(name, source, target):
        reads[name] = pltpu.make_async_copy(source, target, sem.at[len(reads)])
        reads[name].start()

    for i in range(n):
        block = blocks[i]
        halves = i == n - 1 and len(ws) > n
        read(("w", i), ws[i], w_v.at[i, pl.ds(0, 128)] if halves else w_v.at[i])
        if halves:
            read("lower", ws[n], w_v.at[i, pl.ds(128, 128)])
        if i == 0:
            read("cot", cot, cot_v.at[0])
            read("cot_o", cot_o, cot_v.at[1])
        read(("slope", i), rows(slope, block), slope_v.at[i, 0])
        read(("slope_o", i), rows(slope_o, block), slope_v.at[i, 1])
        if i == 0:
            read("inp", inp, inp_v.at[0])
            read("inp_o", inp_o, inp_v.at[1])
        read(("ef", i), rows(ef, block * 2 + core), ef_v.at[i, 0])
        read(("ef_o", i), rows(ef_o, block), ef_v.at[i, 1])

    writes = []
    for i in range(n):
        reads["w", i].wait()
        if i == n - 1 and len(ws) > n:
            reads["lower"].wait()
        hidden = []
        for k, suffix in enumerate(("", "_o")):
            if i == 0:
                reads["cot" + suffix].wait()
            grad_pre = jnp.dot(w_v[i], cot_v[k], preferred_element_type=F32)
            reads["slope" + suffix, i].wait()
            hidden.append((grad_pre * slope_v[i, k].astype(F32)).astype(BF))
        for k, suffix in enumerate(("", "_o")):
            if i == 0:
                reads["inp" + suffix].wait()
            reads["ef" + suffix, i].wait()
        for j in range(4):
            cols = slice(j * 256, (j + 1) * 256)
            total = ef_v[i, 0, :, cols].astype(F32) + ef_v[i, 1, :, cols].astype(F32)
            for k in range(2):
                total += jnp.dot(hidden[k], inp_v[k, :, cols], preferred_element_type=F32)
            total = total.astype(BF)
            for k in range(2):
                out_v[i, 2 * j + k] = total[:, k * 128 : (k + 1) * 128]
            if by_columns:
                writes.append(
                    pltpu.make_async_copy(
                        out_v.at[i, pl.ds(2 * j, 2)], outs[0].at[j, pl.ds(0, 2), i], out_sem.at[len(writes)]
                    )
                )
                writes[-1].start()
        if not by_columns:
            writes.append(pltpu.make_async_copy(out_v.at[i], outs[i], out_sem.at[i]))
            writes[-1].start()
    for write in writes:
        write.wait()


def terms(by_columns, part, here, cot, cot_o, inp, inp_o, slope, slope_o, ef, ef_o, ws):
    n = len(part)
    if by_columns:
        out_shape = [jax.ShapeDtypeStruct((4, 2, n, 256, 128), BF)]
    else:
        out_shape = [jax.ShapeDtypeStruct((8, 256, 128), BF)] * n
    return pl.pallas_call(
        functools.partial(term_kernel, by_columns, part),
        in_specs=[pl.BlockSpec(memory_space=pltpu.SMEM)]
        + [pl.BlockSpec(memory_space=pl.ANY)] * (8 + len(ws)),
        out_specs=[pl.BlockSpec(memory_space=pl.ANY)] * len(out_shape),
        out_shape=out_shape,
        scratch_shapes=[
            pltpu.VMEM((n, 256, 1024), BF),
            pltpu.VMEM((2, 1024, 576), BF),
            pltpu.VMEM((2, 576, 1024), BF),
            pltpu.VMEM((n, 2, 256, 576), BF),
            pltpu.VMEM((n, 2, 256, 1024), BF),
            pltpu.VMEM((n, 8, 256, 128), BF),
            pltpu.SemaphoreType.DMA((5 + 5 * n,)),
            pltpu.SemaphoreType.DMA((4 * n if by_columns else n,)),
        ],
        compiler_params=pltpu.CompilerParams(vmem_limit_bytes=60 * 2**20),
        cost_estimate=pl.CostEstimate(
            flops=(16 if n == 4 else 4) * 1152 * 1024 * 256 * n, bytes_accessed=3 * n * 2**20, transcendentals=0
        ),
    )(here, cot, cot_o, inp, inp_o, slope, slope_o, ef, ef_o, *ws)


def columns_kernel(here, g, out, sem):
    c, _, y, zh = (here[k] for k in range(4))
    copies = []
    for i, dy in enumerate((0, 1, 3, 2)):
        for k in range(2):
            block = lax.rem(y + dy, 4) * 2 + (1 - zh if k else zh)
            cols = pl.ds(pl.multiple_of((2 * block + c) * 256, 256), 256)
            n = 2 * i + k
            copies.append(
                pltpu.make_async_copy(
                    g.at[:, cols], out.at[:, n * 256 : (n + 1) * 256], sem.at[n]
                )
            )
            copies[-1].start()
    for copy in copies:
        copy.wait()


def own_columns(here, g):
    return pl.pallas_call(
        columns_kernel,
        in_specs=[pl.BlockSpec(memory_space=pltpu.SMEM), pl.BlockSpec(memory_space=pl.ANY)],
        out_specs=pl.BlockSpec(memory_space=pltpu.VMEM),
        out_shape=jax.ShapeDtypeStruct((512, 2048), BF),
        scratch_shapes=[pltpu.SemaphoreType.DMA((8,))],
        cost_estimate=pl.CostEstimate(flops=0, bytes_accessed=4 * 2**20, transcendentals=0),
    )(here, g)


def rows_kernel(here, a, out, sem):
    x, zl = here[1], here[4]
    copies = []
    for i, dx in enumerate((0, 1, 3, 2)):
        for k in range(2):
            block = lax.rem(x + dx, 4) * 2 + (1 - zl if k else zl)
            rows = pl.ds(pl.multiple_of(block * 128, 128), 128)
            n = 2 * i + k
            copies.append(
                pltpu.make_async_copy(a.at[rows], out.at[pl.ds(n * 128, 128)], sem.at[n])
            )
            copies[-1].start()
    for copy in copies:
        copy.wait()


def own_rows(here, a):
    return pl.pallas_call(
        rows_kernel,
        in_specs=[pl.BlockSpec(memory_space=pltpu.SMEM), pl.BlockSpec(memory_space=pl.ANY)],
        out_specs=pl.BlockSpec(memory_space=pltpu.VMEM),
        out_shape=jax.ShapeDtypeStruct((1024, 1024), BF),
        scratch_shapes=[pltpu.SemaphoreType.DMA((8,))],
        cost_estimate=pl.CostEstimate(flops=0, bytes_accessed=4 * 2**20, transcendentals=0),
    )(here, a)


def shards(inputs, cotangent, pre_gelu, w_down, error_feedback, a_inverse, g_inverse):
    c, x, y, zh, zl = (lax.axis_index(a) for a in ("c", "x", "y", "zh", "zl"))
    here = jnp.stack([c, x, y, zh, zl]).astype(jnp.int32)

    def swap(a):
        return lax.ppermute(a, "c", [(0, 1), (1, 0)])

    def across_z(a):
        return lax.ppermute(a, ("zl", "zh"), [(i, 3 - i) for i in range(4)])

    def ring(a, axis, step):
        return lax.ppermute(a, axis, [(i, (i + step) % 4) for i in range(4)])

    w_own = lax.dynamic_slice(w_down, (c * 256, 0), (256, 1024))
    first = [ring(w_own, "y", -1), ring(w_own, "y", 1), across_z(w_own)]
    first += [swap(a) for a in (pre_gelu, cotangent)]
    slope, cot, carried = prepare(here, pre_gelu, cotangent, error_feedback)
    g_half = own_columns(here, g_inverse)
    w_up, w_low, w_z, pre_o, cot_o, slope, cot, carried, inp, g_half = lax.optimization_barrier(
        (*first, slope, cot, carried, inputs, g_half)
    )
    upper, lower = cut(w_up, w_low)
    second = [ring(upper, "y", -1), ring(lower, "y", 1), swap(carried), swap(inp)]
    slope_o, cot_o = prepare(here, pre_o, cot_o)
    upper, lower, ef_o, inp_o, slope_o, cot_o, w_up, w_low, w_z = lax.optimization_barrier(
        (*second, slope_o, cot_o, w_up, w_low, w_z)
    )
    third = [ring(w_z, "y", -1), ring(w_z, "y", 1), across_z(upper), across_z(lower)]

    def product(by_columns, part, ws):
        return terms(
            by_columns, part, here, cot, cot_o, inputs, inp_o,
            slope, slope_o, error_feedback, ef_o, ws,
        )

    def added(parts):
        return sum(p.astype(F32) for p in parts).astype(BF)

    def half(a, which):
        return lax.dynamic_index_in_dim(a, which, 0, keepdims=False)

    def exchanged(a, axes):
        return lax.all_to_all(a.reshape(8, 256, 128), axes, 0, 0, tiled=True)

    (near,) = product(True, ((0, 0), (1, 0), (3, 0), (2, 0)), [w_own, w_up, w_low, upper, lower])
    near, third = lax.optimization_barrier((near, third))
    near = added(lax.all_to_all(near, "x", 0, 0, tiled=True))
    near = added([half(near, zl), lax.ppermute(half(near, 1 - zl), "zl", [(0, 1), (1, 0)])])
    near = added([near[0], ring(near[1], "y", 1), ring(near[2], "y", -1), ring(near[3], "y", 2)])
    (far,) = product(False, ((2, 1),), third[2:])
    up, low = product(False, ((1, 1), (3, 1)), [third[0], third[1]])
    (own,) = product(False, ((0, 1),), [w_z])
    own, a_rows = lax.optimization_barrier((own, a_inverse))
    a_rows = own_rows(here, a_rows)
    others = added([own, ring(up, "y", 1), ring(far, "y", 2), ring(low, "y", -1)])
    others, a_rows = lax.optimization_barrier((others, a_rows))
    others = added(exchanged(others, ("x", "zl")))
    theirs = lax.ppermute(jnp.stack([others, near]), "zh", [(0, 1), (1, 0)])
    grad = added([jnp.stack([near, others]), theirs])
    grads = [grad, ring(grad, "y", -1), ring(grad, "y", 1), ring(grad, "y", 2)]
    part = jnp.dot(
        g_half, jnp.concatenate(grads).reshape(2048, 128), preferred_element_type=F32
    ).reshape(2, 256, 128)
    mine, other = (lax.dynamic_index_in_dim(part, k, 0, keepdims=False) for k in (c, 1 - c))
    left = (mine + swap(other)).astype(BF)
    pair = jnp.stack([left, lax.ppermute(left, "zl", [(0, 1), (1, 0)])])
    mine = jnp.concatenate([pair, ring(pair, "x", -1), ring(pair, "x", 1), ring(pair, "x", 2)])
    mine = mine.transpose(1, 0, 2).reshape(256, 1024)
    other = swap(mine)
    both = jnp.where(c == 0, jnp.concatenate([mine, other]), jnp.concatenate([other, mine]))
    return jnp.dot(both, a_rows, preferred_element_type=F32)


def solution(mesh):
    wide = Mesh(mesh.devices.reshape(SIZES), AXES)
    rows, dev = P(AXES, None), P(("y", "zh"), None)
    return jax.shard_map(
        shards,
        mesh=wide,
        in_specs=(rows, rows, rows, dev, rows, P(), dev),
        out_specs=dev,
        check_vma=False,
    )
```

```python
import functools
import math

import jax
import jax.numpy as jnp
from jax import lax
from jax.experimental import pallas as pl
from jax.experimental.pallas import tpu as pltpu
from jax.sharding import Mesh, PartitionSpec as P

AXES = ("zl", "x", "c", "y", "zh")
SIZES = (2, 4, 2, 4, 2)
BF = jnp.bfloat16
F32 = jnp.float32


def gelu_slope(value):
    cdf = 0.5 * (1.0 + lax.erf(value * (1.0 / math.sqrt(2.0))))
    density = jnp.exp(-0.5 * value * value) * (1.0 / math.sqrt(2.0 * math.pi))
    return cdf + value * density


def prepare_kernel(here, pre, cot, *refs):
    with_ef = len(refs) == 11
    ef, (slope, cot_t), carried = refs[0], refs[with_ef : with_ef + 2], refs[3]
    pre_v, cot_v, ef_v, slope_v, cot_tv, sem, out_sem = refs[-7:]
    c = here[0]

    def start(source, target, semaphore):
        copy = pltpu.make_async_copy(source, target, semaphore)
        copy.start()
        return copy

    reads = [
        start(
            pre.at[:, pl.ds(pl.multiple_of((2 * i + c) * 256, 256), 256)], pre_v.at[i], sem.at[i]
        )
        for i in range(8)
    ]
    reads.append(start(cot, cot_v, sem.at[8]))
    if with_ef:
        for i in range(8):
            rows = pl.ds(pl.multiple_of((2 * i + 1 - c) * 256, 256), 256)
            reads.append(start(ef.at[rows], ef_v.at[i], sem.at[9 + i]))
    writes = []

    def write(source, target):
        writes.append(start(source, target, out_sem.at[len(writes)]))

    for i in range(8):
        reads[i].wait()
        slope_v[i] = gelu_slope(pre_v[i].astype(F32)).astype(BF).T
        write(slope_v.at[i], slope.at[pl.ds(i * 256, 256)])
        if with_ef:
            reads[9 + i].wait()
            write(ef_v.at[i], carried.at[pl.ds(i * 256, 256)])
    reads[8].wait()
    cot_tv[...] = cot_v[...].T
    write(cot_tv, cot_t)
    for copy in writes:
        copy.wait()


def prepare(here, pre, cot, ef=None):
    out_shape = [
        jax.ShapeDtypeStruct((2048, 576), BF),
        jax.ShapeDtypeStruct((1024, 576), BF),
    ]
    args = [here, pre, cot]
    if ef is not None:
        args.append(ef)
        out_shape.append(jax.ShapeDtypeStruct((2048, 1024), BF))
    return pl.pallas_call(
        prepare_kernel,
        in_specs=[pl.BlockSpec(memory_space=pltpu.SMEM)]
        + [pl.BlockSpec(memory_space=pl.ANY)] * (len(args) - 1),
        out_specs=[pl.BlockSpec(memory_space=pl.ANY)] * len(out_shape),
        out_shape=out_shape,
        scratch_shapes=[
            pltpu.VMEM((8, 576, 256), BF),
            pltpu.VMEM((576, 1024), BF),
            pltpu.VMEM((8, 256, 1024), BF),
            pltpu.VMEM((8, 256, 576), BF),
            pltpu.VMEM((1024, 576), BF),
            pltpu.SemaphoreType.DMA((17,)),
            pltpu.SemaphoreType.DMA((17,)),
        ],
        compiler_params=pltpu.CompilerParams(vmem_limit_bytes=60 * 2**20),
        cost_estimate=pl.CostEstimate(
            flops=60 * 576 * 2048, bytes_accessed=5 * 2**20, transcendentals=2 * 576 * 2048
        ),
    )(*args)


def cut_kernel(upper, lower, upper_out, lower_out):
    upper_out[...] = upper[...]
    lower_out[...] = lower[...]


def cut(a, b):
    half = (128, 1024)
    return pl.pallas_call(
        cut_kernel,
        grid=(1,),
        in_specs=[pl.BlockSpec(half, lambda i: (0, 0)), pl.BlockSpec(half, lambda i: (1, 0))],
        out_specs=[pl.BlockSpec(half, lambda i: (0, 0))] * 2,
        out_shape=[jax.ShapeDtypeStruct(half, BF)] * 2,
    )(a, b)


def term_kernel(by_columns, part, here, *refs):
    n = len(part)
    cot, cot_o, inp, inp_o, slope, slope_o, ef, ef_o = refs[:8]
    n_out = 1 if by_columns else n
    ws, outs = refs[8 : -8 - n_out], refs[-8 - n_out : -8]
    w_v, cot_v, inp_v, slope_v, ef_v, out_v, sem, out_sem = refs[-8:]
    core, _, y, zh = (here[k] for k in range(4))
    blocks = [lax.rem(y + dy, 4) * 2 + (1 - zh if dz else zh) for dy, dz in part]

    def rows(ref, block):
        return ref.at[pl.ds(pl.multiple_of(block * 256, 256), 256)]

    reads = {}

    def read(name, source, target):
        reads[name] = pltpu.make_async_copy(source, target, sem.at[len(reads)])
        reads[name].start()

    for i in range(n):
        block = blocks[i]
        halves = i == n - 1 and len(ws) > n
        read(("w", i), ws[i], w_v.at[i, pl.ds(0, 128)] if halves else w_v.at[i])
        if halves:
            read("lower", ws[n], w_v.at[i, pl.ds(128, 128)])
        if i == 0:
            read("cot", cot, cot_v.at[0])
            read("cot_o", cot_o, cot_v.at[1])
        read(("slope", i), rows(slope, block), slope_v.at[i, 0])
        read(("slope_o", i), rows(slope_o, block), slope_v.at[i, 1])
        if i == 0:
            read("inp", inp, inp_v.at[0])
            read("inp_o", inp_o, inp_v.at[1])
        read(("ef", i), rows(ef, block * 2 + core), ef_v.at[i, 0])
        read(("ef_o", i), rows(ef_o, block), ef_v.at[i, 1])

    writes = []
    for i in range(n):
        reads["w", i].wait()
        if i == n - 1 and len(ws) > n:
            reads["lower"].wait()
        hidden = []
        for k, suffix in enumerate(("", "_o")):
            if i == 0:
                reads["cot" + suffix].wait()
            grad_pre = jnp.dot(w_v[i], cot_v[k], preferred_element_type=F32)
            reads["slope" + suffix, i].wait()
            hidden.append((grad_pre * slope_v[i, k].astype(F32)).astype(BF))
        for k, suffix in enumerate(("", "_o")):
            if i == 0:
                reads["inp" + suffix].wait()
            reads["ef" + suffix, i].wait()
        for j in range(4):
            cols = slice(j * 256, (j + 1) * 256)
            total = ef_v[i, 0, :, cols].astype(F32) + ef_v[i, 1, :, cols].astype(F32)
            for k in range(2):
                total += jnp.dot(hidden[k], inp_v[k, :, cols], preferred_element_type=F32)
            total = total.astype(BF)
            for k in range(2):
                out_v[i, 2 * j + k] = total[:, k * 128 : (k + 1) * 128]
            if by_columns:
                writes.append(
                    pltpu.make_async_copy(
                        out_v.at[i, pl.ds(2 * j, 2)], outs[0].at[j, pl.ds(0, 2), i], out_sem.at[len(writes)]
                    )
                )
                writes[-1].start()
        if not by_columns:
            writes.append(pltpu.make_async_copy(out_v.at[i], outs[i], out_sem.at[i]))
            writes[-1].start()
    for write in writes:
        write.wait()


def terms(by_columns, part, here, cot, cot_o, inp, inp_o, slope, slope_o, ef, ef_o, ws):
    n = len(part)
    if by_columns:
        out_shape = [jax.ShapeDtypeStruct((4, 2, n, 256, 128), BF)]
    else:
        out_shape = [jax.ShapeDtypeStruct((8, 256, 128), BF)] * n
    return pl.pallas_call(
        functools.partial(term_kernel, by_columns, part),
        in_specs=[pl.BlockSpec(memory_space=pltpu.SMEM)]
        + [pl.BlockSpec(memory_space=pl.ANY)] * (8 + len(ws)),
        out_specs=[pl.BlockSpec(memory_space=pl.ANY)] * len(out_shape),
        out_shape=out_shape,
        scratch_shapes=[
            pltpu.VMEM((n, 256, 1024), BF),
            pltpu.VMEM((2, 1024, 576), BF),
            pltpu.VMEM((2, 576, 1024), BF),
            pltpu.VMEM((n, 2, 256, 576), BF),
            pltpu.VMEM((n, 2, 256, 1024), BF),
            pltpu.VMEM((n, 8, 256, 128), BF),
            pltpu.SemaphoreType.DMA((5 + 5 * n,)),
            pltpu.SemaphoreType.DMA((4 * n if by_columns else n,)),
        ],
        compiler_params=pltpu.CompilerParams(vmem_limit_bytes=60 * 2**20),
        cost_estimate=pl.CostEstimate(
            flops=(16 if n == 4 else 4) * 1152 * 1024 * 256 * n, bytes_accessed=3 * n * 2**20, transcendentals=0
        ),
    )(here, cot, cot_o, inp, inp_o, slope, slope_o, ef, ef_o, *ws)


def columns_kernel(here, g, out, sem):
    c, _, y, zh = (here[k] for k in range(4))
    copies = []
    for i, dy in enumerate((0, 1, 3, 2)):
        for k in range(2):
            block = lax.rem(y + dy, 4) * 2 + (1 - zh if k else zh)
            cols = pl.ds(pl.multiple_of((2 * block + c) * 256, 256), 256)
            n = 2 * i + k
            copies.append(
                pltpu.make_async_copy(
                    g.at[:, cols], out.at[:, n * 256 : (n + 1) * 256], sem.at[n]
                )
            )
            copies[-1].start()
    for copy in copies:
        copy.wait()


def own_columns(here, g):
    return pl.pallas_call(
        columns_kernel,
        in_specs=[pl.BlockSpec(memory_space=pltpu.SMEM), pl.BlockSpec(memory_space=pl.ANY)],
        out_specs=pl.BlockSpec(memory_space=pltpu.VMEM),
        out_shape=jax.ShapeDtypeStruct((512, 2048), BF),
        scratch_shapes=[pltpu.SemaphoreType.DMA((8,))],
        cost_estimate=pl.CostEstimate(flops=0, bytes_accessed=4 * 2**20, transcendentals=0),
    )(here, g)


def shards(inputs, cotangent, pre_gelu, w_down, error_feedback, a_inverse, g_inverse):
    c, x, y, zh, zl = (lax.axis_index(a) for a in ("c", "x", "y", "zh", "zl"))
    here = jnp.stack([c, x, y, zh]).astype(jnp.int32)

    def swap(a):
        return lax.ppermute(a, "c", [(0, 1), (1, 0)])

    def across_z(a):
        return lax.ppermute(a, ("zl", "zh"), [(i, 3 - i) for i in range(4)])

    def ring(a, axis, step):
        return lax.ppermute(a, axis, [(i, (i + step) % 4) for i in range(4)])

    w_own = lax.dynamic_slice(w_down, (c * 256, 0), (256, 1024))
    first = [ring(w_own, "y", -1), ring(w_own, "y", 1), across_z(w_own)]
    first += [swap(a) for a in (pre_gelu, cotangent)]
    slope, cot, carried = prepare(here, pre_gelu, cotangent, error_feedback)
    g_half = own_columns(here, g_inverse)
    w_up, w_low, w_z, pre_o, cot_o, slope, cot, carried, inp, g_half = lax.optimization_barrier(
        (*first, slope, cot, carried, inputs, g_half)
    )
    upper, lower = cut(w_up, w_low)
    second = [ring(upper, "y", -1), ring(lower, "y", 1), swap(carried), swap(inp)]
    slope_o, cot_o = prepare(here, pre_o, cot_o)
    upper, lower, ef_o, inp_o, slope_o, cot_o, w_up, w_low, w_z = lax.optimization_barrier(
        (*second, slope_o, cot_o, w_up, w_low, w_z)
    )
    third = [ring(w_z, "y", -1), ring(w_z, "y", 1), across_z(upper), across_z(lower)]

    def product(by_columns, part, ws):
        return terms(
            by_columns, part, here, cot, cot_o, inputs, inp_o,
            slope, slope_o, error_feedback, ef_o, ws,
        )

    def added(parts):
        return sum(p.astype(F32) for p in parts).astype(BF)

    def half(a, which):
        return lax.dynamic_index_in_dim(a, which, 0, keepdims=False)

    def exchanged(a, axes):
        return lax.all_to_all(a.reshape(8, 256, 128), axes, 0, 0, tiled=True)

    (near,) = product(True, ((0, 0), (1, 0), (3, 0), (2, 0)), [w_own, w_up, w_low, upper, lower])
    near, third = lax.optimization_barrier((near, third))
    near = added(lax.all_to_all(near, "x", 0, 0, tiled=True))
    near = added([half(near, zl), lax.ppermute(half(near, 1 - zl), "zl", [(0, 1), (1, 0)])])
    near = added([near[0], ring(near[1], "y", 1), ring(near[2], "y", -1), ring(near[3], "y", 2)])
    (far,) = product(False, ((2, 1),), third[2:])
    up, low = product(False, ((1, 1), (3, 1)), [third[0], third[1]])
    (own,) = product(False, ((0, 1),), [w_z])
    others = added([own, ring(up, "y", 1), ring(far, "y", 2), ring(low, "y", -1)])
    others = added(exchanged(others, ("x", "zl")))
    theirs = lax.ppermute(jnp.stack([others, near]), "zh", [(0, 1), (1, 0)])
    grad = added([jnp.stack([near, others]), theirs])
    grads = [grad, ring(grad, "y", -1), ring(grad, "y", 1), ring(grad, "y", 2)]
    part = jnp.dot(g_half[:, :512], grad.reshape(512, 128), preferred_element_type=F32)
    part += jnp.dot(
        g_half[:, 512:], jnp.concatenate(grads[1:]).reshape(1536, 128), preferred_element_type=F32
    )
    part = part.reshape(2, 256, 128)
    mine, other = (lax.dynamic_index_in_dim(part, k, 0, keepdims=False) for k in (c, 1 - c))
    left = (mine + swap(other)).astype(BF)
    mine = lax.all_to_all(
        jnp.broadcast_to(left[None], (8, 256, 128)), ("x", "zl"), 0, 0, tiled=True
    ).transpose(1, 0, 2).reshape(256, 1024)
    other = swap(mine)
    both = jnp.where(c == 0, jnp.concatenate([mine, other]), jnp.concatenate([other, mine]))
    return jnp.dot(both, a_inverse, preferred_element_type=F32)


def solution(mesh):
    wide = Mesh(mesh.devices.reshape(SIZES), AXES)
    rows, dev = P(AXES, None), P(("y", "zh"), None)
    return jax.shard_map(
        shards,
        mesh=wide,
        in_specs=(rows, rows, rows, dev, rows, P(), dev),
        out_specs=dev,
        check_vma=False,
    )
```
